256 devices in a mesh: dp: 8 (over x, core), seq: 32 (over y, z).
Axes of the slice: x: 4, y: 4, z: 8, core: 2. Of those that a mesh axis runs over, the one named last changes fastest.
Arguments:
- probe_vectors: float32 [8, 4096, 2048], P('dp', 'seq'), may hold values from -8 to 8
- lookup_vectors: float32 [8, 4096, 2048], P('dp', 'seq'), may hold values from -8 to 8
- payload_vectors: float32 [8, 4096, 2048], P('dp', 'seq'), may hold values from -8 to 8
- channel_sharpness: float32 [16], replicated, may hold values from 0.7 to 1.4
- adjacent_tiles: int32 [8, 32, 4], P('dp'), may hold values from 0 to 31, as said below
- output_adjoint: float32 [8, 4096, 2048], P('dp', 'seq'), may hold values from -16 to 16
Outputs:
- context_output: float32 [8, 4096, 2048], P('dp', 'seq')
- probe_derivative: float32 [8, 4096, 2048], P('dp', 'seq')
- lookup_derivative: float32 [8, 4096, 2048], P('dp', 'seq')
- payload_derivative: float32 [8, 4096, 2048], P('dp', 'seq')
- channel_sharpness_derivative: float32 [16], replicated
The draws below stay inside these ranges and needn't reach their ends.
Inputs may be any that keep to these rules, and one draw needn't show every extreme that they name: `adjacent_tiles`: row b of each sequence lists b first, then b - 1 and b + 1 modulo 32, then one further block; the 4 entries of a row are distinct.
All inputs are finite; a program needn't handle non-finite values.
Results may differ from the reference program's by a relative error of at most 0.0003.
Values sent between devices are 32-bit elements; how exact they have to be, the bound alone decides.
A program may use at most 128 MiB of HBM per device.

```python
import math
import jax
import jax.numpy as jnp
from jax import lax

RESIDENT_CHANNELS = 16
HD = 128
BLOCK = 128
NB = 4
NBLK = 32
LEN = 4096
GROUPS = 8
HW = 2048


def draw_probe_vectors(key, part):
    own_key = jax.random.fold_in(key, 1)
    shape = (GROUPS, NBLK, BLOCK, RESIDENT_CHANNELS * HD)
    base = jnp.clip(jax.random.normal(own_key, shape, jnp.float32), -8.0, 8.0)
    return base.reshape(GROUPS, NBLK * BLOCK, RESIDENT_CHANNELS * HD)


def draw_lookup_vectors(key, part):
    own_key = jax.random.fold_in(key, 2)
    shape = (GROUPS, NBLK, BLOCK, RESIDENT_CHANNELS * HD)
    base = jnp.clip(jax.random.normal(own_key, shape, jnp.float32), -8.0, 8.0)
    return base.reshape(GROUPS, NBLK * BLOCK, RESIDENT_CHANNELS * HD)


def draw_output_adjoint(key, part):
    own_key = jax.random.fold_in(key, 3)
    shape = (GROUPS, NBLK * BLOCK, RESIDENT_CHANNELS * HD)
    group_index = jnp.arange(GROUPS).reshape(GROUPS, 1, 1).astype(jnp.float32)
    token_index = jnp.arange(NBLK * BLOCK).reshape(1, NBLK * BLOCK, 1).astype(jnp.float32)
    fraction = (group_index * (NBLK * BLOCK) + token_index) / (GROUPS * NBLK * BLOCK - 1)
    base = jnp.clip(jax.random.normal(own_key, shape, jnp.float32), -4.0, 4.0)
    return base * (1.0 + 2.0 * fraction)


def draw_adjacent_tiles(key, part):
    own_key = jax.random.fold_in(key, 4)
    popular = jax.random.randint(jax.random.fold_in(own_key, 1), (GROUPS, 1, NBLK), 0, 1 << 15, jnp.int32)
    jitter = jax.random.randint(jax.random.fold_in(own_key, 2), (GROUPS, NBLK, NBLK), 0, 1 << 14, jnp.int32)
    blocks = jnp.arange(NBLK, dtype=jnp.int32)
    scores = (popular + jitter) * NBLK + blocks.reshape(1, 1, NBLK)
    rows = blocks.reshape(NBLK, 1)
    cols = blocks.reshape(1, NBLK)
    before = (rows + NBLK - 1) % NBLK
    after = (rows + 1) % NBLK
    window = (cols == rows) | (cols == before) | (cols == after)
    scores = jnp.where(window.reshape(1, NBLK, NBLK), -1, scores)
    ranked, picked = lax.top_k(scores, NB - 3)
    front = jnp.concatenate([rows, before, after], axis=1)
    front = jnp.broadcast_to(front.reshape(1, NBLK, 3), (GROUPS, NBLK, 3))
    return jnp.concatenate([front, picked.astype(jnp.int32)], axis=2).astype(jnp.int32)


def level_of(key, dims, pieces, smallest, high):
    factor_of, own = 1.0, jax.random.fold_in(key, 6)
    for position, blocks in pieces:
        steps = jnp.exp(jax.random.uniform(jax.random.fold_in(own, position), (blocks,), jnp.float32, smallest / len(pieces), high / len(pieces)))
        factor_of = factor_of * jnp.repeat(steps, dims[position] // blocks).reshape([-1 if axis == position else 1 for axis in range(len(dims))])
    return factor_of


def noise(stream_key, dims, spread, most, shards=(), kind=jnp.bfloat16):
    factor_of = level_of(stream_key, dims, shards, -0.22, 0.18) if shards else 1.0
    result = jax.random.normal(stream_key, dims, jnp.float32) * spread * factor_of
    return jnp.minimum(jnp.maximum(result, -most), most).astype(kind)


def setup_inputs(seed: int = 0) -> dict:
    key_list = jax.random.split(jax.random.key(seed), 7)
    probe_vectors = draw_probe_vectors(jax.random.fold_in(key_list[6], 71), 0)
    lookup_vectors = draw_lookup_vectors(jax.random.fold_in(key_list[6], 71), 0)
    payload_vectors = noise(key_list[2], (GROUPS, LEN, HW), 1.0, 8.0, ((0, 8), (1, 32)), jnp.float32)
    channel_sharpness = jnp.clip(jnp.exp(jax.random.uniform(key_list[3], (RESIDENT_CHANNELS,), jnp.float32, math.log(0.7), math.log(1.4))), 0.7, 1.4)
    adjacent_tiles = draw_adjacent_tiles(jax.random.fold_in(key_list[6], 71), 0)
    output_adjoint = draw_output_adjoint(jax.random.fold_in(key_list[6], 71), 0)
    return dict(probe_vectors=probe_vectors, lookup_vectors=lookup_vectors, payload_vectors=payload_vectors, channel_sharpness=channel_sharpness, adjacent_tiles=adjacent_tiles, output_adjoint=output_adjoint)


def bucketed_contributions(probe_vector_lines, lookup_vector_lines, payload_vector_lines, channel_sharpness, adjacent_tile_lines, incoming_adjoint_lines):
    reciprocal_dimension_sqrt = 1.0 / math.sqrt(HD)

    def primal_evaluation(probe_vector_lines, lookup_vector_lines, payload_vector_lines, channel_sharpness):
        query_heads = probe_vector_lines.reshape(-1, BLOCK, RESIDENT_CHANNELS, HD)
        key_heads = lookup_vector_lines.reshape(-1, BLOCK, RESIDENT_CHANNELS, HD)
        value_heads = payload_vector_lines.reshape(-1, BLOCK, RESIDENT_CHANNELS, HD)

        def one_block(pair):
            query_block, listed_row = pair
            listed_keys = jnp.take(key_heads, listed_row, axis=0).reshape(NB * BLOCK, RESIDENT_CHANNELS, HD)
            listed_values = jnp.take(value_heads, listed_row, axis=0).reshape(NB * BLOCK, RESIDENT_CHANNELS, HD)
            plain_logits = jnp.einsum('qhd,khd->hqk', query_block, listed_keys, precision=lax.Precision.HIGHEST) * reciprocal_dimension_sqrt
            normalized_probabilities = jax.nn.softmax(channel_sharpness[:, None, None] * plain_logits, axis=-1)
            return jnp.einsum('hqk,khd->qhd', normalized_probabilities, listed_values, precision=lax.Precision.HIGHEST)
        context_output = lax.map(one_block, (query_heads, adjacent_tile_lines))
        return context_output.reshape(probe_vector_lines.shape)
    context_output, reverse_mode_rule = jax.vjp(primal_evaluation, probe_vector_lines, lookup_vector_lines, payload_vector_lines, channel_sharpness)
    grads = reverse_mode_rule(incoming_adjoint_lines)
    return (context_output, grads[0], grads[1], grads[2], grads[3])

def reference(probe_vectors, lookup_vectors, payload_vectors, channel_sharpness, adjacent_tiles, output_adjoint):

    def per_group(coordinate_couples):
        return bucketed_contributions(coordinate_couples[0], coordinate_couples[1], coordinate_couples[2], channel_sharpness, coordinate_couples[3], coordinate_couples[4])
    outcome_tuple = lax.map(per_group, (probe_vectors, lookup_vectors, payload_vectors, adjacent_tiles, output_adjoint))
    context_output, probe_derivative, lookup_derivative, payload_derivative, sharpness_contributions = outcome_tuple
    return (context_output, probe_derivative, lookup_derivative, payload_derivative, lax.optimization_barrier(jnp.sum(sharpness_contributions, axis=0)))
```

```python
import functools
import math

import jax
import jax.numpy as jnp
from jax import lax
from jax.experimental import pallas as pl
from jax.experimental.pallas import tpu as pltpu
from jax.sharding import PartitionSpec as P

HD = 128
BLOCK = 128
NB = 4
MESH = pl.DeviceIdType.MESH
HIGH = lax.Precision.HIGHEST


def dot(a, b, ca, cb):
    return lax.dot_general(
        a, b, (((ca,), (cb,)), ((), ())), precision=HIGH, preferred_element_type=jnp.float32
    )


def kernel(
    chips,
    dps,
    q_ref,
    k_ref,
    v_ref,
    g_ref,
    adj_ref,
    sharp_ref,
    o_ref,
    dq_ref,
    dk_ref,
    dv_ref,
    ds_ref,
    kx,
    vx,
    qg,
    oq,
    dk,
    dv,
    runk,
    runv,
    part,
    adjv,
    adjs,
    prevs,
    lasts,
    sh_own,
    sh_sib,
    sh_tot,
    sh_all,
    dp_all,
    send_in,
    send_relay,
    send_oq,
    send_dkv,
    send_part,
    send_small,
    recv_kv,
    recv_q,
    recv_relay,
    recv_part,
    recv_out,
    recv_small,
):
    heads = chips // 2
    dp = lax.axis_index("dp")
    c = lax.axis_index("seq")
    X2 = (dp // 2) * 2
    s = dp % 2
    p = c % 2
    head = c // 2
    same = p == s
    sibling = (X2 + 1 - s, c)

    def partner(i):
        return (X2 + p, 2 * i + s)

    def is_self(i):
        return jnp.logical_and(same, 2 * i + s == c)

    barrier = pltpu.get_barrier_semaphore()

    def greet(i, _):
        @pl.when(jnp.logical_not(is_self(i)))
        def _():
            pl.semaphore_signal(barrier, inc=1, device_id=partner(i), device_id_type=MESH)

        return _

    lax.fori_loop(0, heads, greet, None)

    def greet_dp(i, _):
        @pl.when(i != dp)
        def _():
            pl.semaphore_signal(barrier, inc=1, device_id=(i, c), device_id_type=MESH)

        return _

    lax.fori_loop(0, dps, greet_dp, None)
    pl.semaphore_wait(barrier, jnp.where(same, heads - 1, heads) + dps - 1)

    def put(i, src, dst, send, recv):
        @pl.when(is_self(i))
        def _():
            pltpu.make_async_copy(src, dst, recv).start()

        @pl.when(jnp.logical_not(is_self(i)))
        def _():
            pltpu.make_async_remote_copy(
                src, dst, send, recv, device_id=partner(i), device_id_type=MESH
            ).start()

    def columns(ref, h):
        return ref.at[:, pl.ds(pl.multiple_of(h * HD, HD), HD)]

    def to_sibling(src, dst, send, recv):
        return pltpu.make_async_remote_copy(
            src, dst, send, recv, device_id=sibling, device_id_type=MESH
        )

    adj_copy = to_sibling(adj_ref, adjv.at[1], send_small.at[0], recv_small.at[0])
    adj_copy.start()
    own_adj = pltpu.make_async_copy(adj_ref, adjv.at[0], recv_small.at[1])
    own_adj.start()

    def send_k(t, _):
        h = lax.rem(head + t, heads)
        put(h, columns(k_ref, h), kx.at[p, head], send_in, recv_kv.at[0])
        return _

    def send_v(t, _):
        h = lax.rem(head + t, heads)
        put(h, columns(v_ref, h), vx.at[p, head], send_in, recv_kv.at[1])
        return _

    def send_q(t, _):
        h = lax.rem(head + t, heads)
        put(h, columns(q_ref, h), qg.at[head, 0], send_in, recv_q.at[head])
        put(h, columns(g_ref, h), qg.at[head, 1], send_in, recv_q.at[head])
        return _

    lax.fori_loop(0, heads, send_k, None)
    lax.fori_loop(0, heads, send_v, None)
    lax.fori_loop(0, heads, send_q, None)

    adj_copy.wait()
    own_adj.wait()
    to_scalars = pltpu.make_async_copy(adjv.at[jnp.where(same, 0, 1)], adjs, recv_small.at[1])
    to_scalars.start()
    to_scalars.wait()

    def slot_of(t):
        return lax.rem(head - t + heads, heads)

    def far_of(t):
        return adjs[0, (2 * slot_of(t) + s) * NB + NB - 1]

    def chain(t, _):
        mine = far_of(t)

        def look(u, found):
            return jnp.where(jnp.logical_and(u < t, far_of(u) == mine), u, found)

        prevs[t] = lax.fori_loop(0, heads, look, jnp.int32(-1))
        return _

    lax.fori_loop(0, heads, chain, None)

    def last_of(k, _):
        def look(u, found):
            return jnp.where(far_of(u) == k, u, found)

        lasts[k] = lax.fori_loop(0, heads, look, jnp.int32(-1))
        return _

    lax.fori_loop(0, chips, last_of, None)

    def clear(i, _):
        dk[0, i, :, :] = jnp.zeros((BLOCK, HD), jnp.float32)
        dk[1, i, :, :] = jnp.zeros((BLOCK, HD), jnp.float32)
        dv[0, i, :, :] = jnp.zeros((BLOCK, HD), jnp.float32)
        dv[1, i, :, :] = jnp.zeros((BLOCK, HD), jnp.float32)
        return _

    lax.fori_loop(0, heads, clear, None)

    for i, ref in enumerate((kx, vx)):
        pltpu.make_async_copy(ref.at[s], ref.at[s], recv_kv.at[i]).wait()
        to_sibling(ref.at[s], ref.at[s], send_relay.at[i], recv_relay.at[i]).start()
    for i, ref in enumerate((kx, vx)):
        pltpu.make_async_copy(ref.at[1 - s], ref.at[1 - s], recv_relay.at[i]).wait()

    sharp = sharp_ref[head]
    scale = sharp * (1.0 / math.sqrt(HD))

    def step(t, acc):
        j = slot_of(t)
        b = 2 * j + s
        pltpu.make_async_copy(qg.at[j], qg.at[j], recv_q.at[j]).wait()
        q = qg[j, 0] * scale
        g = qg[j, 1]
        far = far_of(t)
        before = lax.rem(b + chips - 1, chips)
        after = lax.rem(b + 1, chips)

        def listed(ref):
            return jnp.concatenate(
                [ref[s, j], ref[1 - s, before // 2], ref[1 - s, after // 2], ref[far % 2, far // 2]],
                axis=0,
            )

        keys = listed(kx)
        values = listed(vx)
        logits = dot(keys, q, 1, 1)
        prob_grad = dot(values, g, 1, 1)
        top = jnp.max(logits, axis=0, keepdims=True)
        shifted = jnp.exp(logits - top)
        prob = shifted * (1.0 / jnp.sum(shifted, axis=0, keepdims=True))
        row_dot = jnp.sum(prob * prob_grad, axis=0, keepdims=True)
        score_grad = prob * (prob_grad - row_dot)
        acc = acc + jnp.sum(score_grad * logits, axis=0, keepdims=True)
        oq[j, 0] = dot(prob, values, 0, 0)
        oq[j, 1] = dot(score_grad, keys, 0, 0) * scale
        put(j, oq.at[j, 0], columns(o_ref, head), send_oq, recv_out.at[0])
        put(j, oq.at[j, 1], columns(dq_ref, head), send_oq, recv_out.at[1])
        key_terms = dot(score_grad, q, 1, 0)
        value_terms = dot(prob, g, 1, 0)
        back = prevs[t]
        at = jnp.maximum(back, 0)
        for total, run, terms in ((dk, runk, key_terms), (dv, runv, value_terms)):
            total[s, j] += terms[:BLOCK]
            total[1 - s, before // 2] += terms[BLOCK : 2 * BLOCK]
            total[1 - s, after // 2] += terms[2 * BLOCK : 3 * BLOCK]
            run[t] = terms[3 * BLOCK :] + jnp.where(back >= 0, run[at], 0.0)
        return acc

    acc = lax.fori_loop(0, heads, step, jnp.zeros((1, HD), jnp.float32))

    sh_own[...] = jnp.broadcast_to(jnp.sum(acc, axis=1, keepdims=True) / sharp, (8, HD))
    small = to_sibling(sh_own, sh_sib, send_small.at[1], recv_small.at[2])
    small.start()

    def gather(total, run, half, i):
        at = lasts[2 * i + half]
        return total[half, i] + jnp.where(at >= 0, run[jnp.maximum(at, 0)], 0.0)

    def far_sibling(i, _):
        dk[1 - s, i] = gather(dk, runk, 1 - s, i)
        dv[1 - s, i] = gather(dv, runv, 1 - s, i)
        return _

    lax.fori_loop(0, heads, far_sibling, None)
    for i, ref in enumerate((dk, dv)):
        to_sibling(ref.at[1 - s], part.at[i], send_part.at[i], recv_part.at[i]).start()

    small.wait()
    sh_tot[...] = sh_own[...] + sh_sib[...]

    def send_sharp(i, _):
        put(i, sh_tot, sh_all.at[head], send_small.at[2], recv_small.at[3])
        return _

    lax.fori_loop(0, heads, send_sharp, None)

    for i in range(2):
        pltpu.make_async_copy(part.at[i], part.at[i], recv_part.at[i]).wait()

    def finish(t, _):
        j = slot_of(t)
        dk[s, j] = gather(dk, runk, s, j) + part[0, j]
        dv[s, j] = gather(dv, runv, s, j) + part[1, j]
        put(j, dk.at[s, j], columns(dk_ref, head), send_dkv, recv_out.at[2])
        put(j, dv.at[s, j], columns(dv_ref, head), send_dkv, recv_out.at[3])
        return _

    lax.fori_loop(0, heads, finish, None)

    pltpu.make_async_copy(sh_all, sh_all, recv_small.at[3]).wait()
    dp_all[dp] = sh_all[:, 0, :]

    def send_dp(i, _):
        @pl.when(i != dp)
        def _():
            pltpu.make_async_remote_copy(
                dp_all.at[dp],
                dp_all.at[dp],
                send_small.at[3],
                recv_small.at[4],
                device_id=(i, c),
                device_id_type=MESH,
            ).start()

        return _

    lax.fori_loop(0, dps, send_dp, None)
    others = dp_all.at[pl.ds(0, dps - 1)]
    pltpu.make_async_copy(others, others, recv_small.at[4]).wait()
    total = dp_all[0]
    for i in range(1, dps):
        total = total + dp_all[i]
    ds_ref[...] = total

    pltpu.make_async_copy(others, others, send_small.at[3]).wait()
    for i, ref in enumerate((kx, vx)):
        pltpu.make_async_copy(ref.at[s], ref.at[s], send_relay.at[i]).wait()
    for i in range(2):
        pltpu.make_async_copy(part.at[i], part.at[i], send_part.at[i]).wait()

    def drain(count):
        few = qg.at[pl.ds(0, count)]
        pltpu.make_async_copy(few, few, send_in).wait()
        pltpu.make_async_copy(few, few, send_in).wait()
        pltpu.make_async_copy(few, few, send_oq).wait()
        pltpu.make_async_copy(few, few, send_dkv).wait()
        tiles = sh_all.at[pl.ds(0, count)]
        pltpu.make_async_copy(tiles, tiles, send_small.at[2]).wait()

    @pl.when(same)
    def _():
        drain(heads - 1)

    @pl.when(jnp.logical_not(same))
    def _():
        drain(heads)

    for i, ref in enumerate((o_ref, dq_ref, dk_ref, dv_ref)):
        pltpu.make_async_copy(ref, ref, recv_out.at[i]).wait()


def per_device(queries, keys, values, sharpness, listing, adjoint):
    chips = lax.axis_size("seq")
    dps = lax.axis_size("dp")
    heads = chips // 2
    rows, features = queries.shape[1:]
    f32 = jnp.float32
    anywhere = pl.BlockSpec(memory_space=pl.ANY)
    block = (BLOCK, HD)
    whole = jax.ShapeDtypeStruct((rows, features), f32)
    dma = pltpu.SemaphoreType.DMA
    o, dq, dk, dv, ds = pl.pallas_call(
        functools.partial(kernel, chips, dps),
        out_shape=[whole] * 4 + [jax.ShapeDtypeStruct((heads, HD), f32)],
        in_specs=[anywhere] * 5 + [pl.BlockSpec(memory_space=pltpu.SMEM)],
        out_specs=[anywhere] * 4 + [pl.BlockSpec(memory_space=pltpu.VMEM)],
        scratch_shapes=[
            pltpu.VMEM((2, heads) + block, f32),
            pltpu.VMEM((2, heads) + block, f32),
            pltpu.VMEM((heads, 2) + block, f32),
            pltpu.VMEM((heads, 2) + block, f32),
            pltpu.VMEM((2, heads) + block, f32),
            pltpu.VMEM((2, heads) + block, f32),
            pltpu.VMEM((heads,) + block, f32),
            pltpu.VMEM((heads,) + block, f32),
            pltpu.VMEM((2, heads) + block, f32),
            pltpu.VMEM((2, 1, chips * NB), jnp.int32),
            pltpu.SMEM((1, chips * NB), jnp.int32),
            pltpu.SMEM((heads,), jnp.int32),
            pltpu.SMEM((chips,), jnp.int32),
            pltpu.VMEM((8, HD), f32),
            pltpu.VMEM((8, HD), f32),
            pltpu.VMEM((8, HD), f32),
            pltpu.VMEM((heads, 8, HD), f32),
            pltpu.VMEM((dps, heads, HD), f32),
            dma,
            dma((2,)),
            dma,
            dma,
            dma((2,)),
            dma((4,)),
            dma((2,)),
            dma((heads,)),
            dma((2,)),
            dma((2,)),
            dma((4,)),
            dma((5,)),
        ],
        compiler_params=pltpu.CompilerParams(
            collective_id=0, has_side_effects=True, vmem_limit_bytes=48 * 2**20
        ),
        name="attend",
    )(
        queries[0],
        keys[0],
        values[0],
        adjoint[0],
        listing.reshape(1, chips * NB),
        sharpness,
    )
    return o[None], dq[None], dk[None], dv[None], ds[:, 0]


def solution(mesh):
    tokens = P("dp", "seq", None)
    return jax.shard_map(
        per_device,
        mesh=mesh,
        in_specs=(tokens, tokens, tokens, P(), P("dp", None, None), tokens),
        out_specs=(tokens, tokens, tokens, tokens, P()),
        check_vma=False,
    )
```

```python
import functools
import math

import jax
import jax.numpy as jnp
from jax import lax
from jax.experimental import pallas as pl
from jax.experimental.pallas import tpu as pltpu
from jax.sharding import PartitionSpec as P

HD = 128
BLOCK = 128
NB = 4
MESH = pl.DeviceIdType.MESH
HIGH = lax.Precision.HIGHEST


def dot(a, b, ca, cb):
    return lax.dot_general(
        a, b, (((ca,), (cb,)), ((), ())), precision=HIGH, preferred_element_type=jnp.float32
    )


def kernel(
    chips,
    dps,
    q_ref,
    k_ref,
    v_ref,
    g_ref,
    adj_ref,
    sharp_ref,
    o_ref,
    dq_ref,
    dk_ref,
    dv_ref,
    ds_ref,
    kx,
    vx,
    qg,
    oq,
    dk,
    dv,
    runk,
    runv,
    part,
    adjv,
    adjs,
    sharps,
    prevs,
    lasts,
    sh_own,
    sh_sib,
    sh_tot,
    sh_all,
    dp_all,
    send_in,
    send_relay,
    send_oq,
    send_dkv,
    send_part,
    send_small,
    recv_kv,
    recv_q,
    recv_relay,
    recv_part,
    recv_out,
    recv_small,
):
    heads = chips // 2
    dp = lax.axis_index("dp")
    c = lax.axis_index("seq")
    X2 = (dp // 2) * 2
    s = dp % 2
    p = c % 2
    head = c // 2
    same = p == s
    sibling = (X2 + 1 - s, c)

    def partner(i):
        return (X2 + p, 2 * i + s)

    def is_self(i):
        return jnp.logical_and(same, 2 * i + s == c)

    barrier = pltpu.get_barrier_semaphore()

    def greet(i, _):
        @pl.when(jnp.logical_not(is_self(i)))
        def _():
            pl.semaphore_signal(barrier, inc=1, device_id=partner(i), device_id_type=MESH)

        return _

    lax.fori_loop(0, heads, greet, None)

    def greet_dp(i, _):
        @pl.when(i != dp)
        def _():
            pl.semaphore_signal(barrier, inc=1, device_id=(i, c), device_id_type=MESH)

        return _

    lax.fori_loop(0, dps, greet_dp, None)
    pl.semaphore_wait(barrier, jnp.where(same, heads - 1, heads) + dps - 1)

    def put(i, src, dst, send, recv):
        @pl.when(is_self(i))
        def _():
            pltpu.make_async_copy(src, dst, recv).start()

        @pl.when(jnp.logical_not(is_self(i)))
        def _():
            pltpu.make_async_remote_copy(
                src, dst, send, recv, device_id=partner(i), device_id_type=MESH
            ).start()

    def columns(ref, h):
        return ref.at[:, pl.ds(pl.multiple_of(h * HD, HD), HD)]

    def to_sibling(src, dst, send, recv):
        return pltpu.make_async_remote_copy(
            src, dst, send, recv, device_id=sibling, device_id_type=MESH
        )

    adj_copy = to_sibling(adj_ref, adjv.at[1], send_small.at[0], recv_small.at[0])
    adj_copy.start()
    own_adj = pltpu.make_async_copy(adj_ref, adjv.at[0], recv_small.at[1])
    own_adj.start()
    own_sharp = pltpu.make_async_copy(sharp_ref, sharps, recv_small.at[5])
    own_sharp.start()

    def send_k(t, _):
        h = lax.rem(head + t, heads)
        put(h, columns(k_ref, h), kx.at[p, head], send_in, recv_kv.at[0])
        return _

    def send_v(t, _):
        h = lax.rem(head + t, heads)
        put(h, columns(v_ref, h), vx.at[p, head], send_in, recv_kv.at[1])
        return _

    def send_q(t, _):
        h = lax.rem(head + t, heads)
        put(h, columns(q_ref, h), qg.at[head, 0], send_in, recv_q.at[head])
        put(h, columns(g_ref, h), qg.at[head, 1], send_in, recv_q.at[head])
        return _

    lax.fori_loop(0, heads, send_k, None)
    lax.fori_loop(0, heads, send_v, None)
    lax.fori_loop(0, heads, send_q, None)

    adj_copy.wait()
    own_adj.wait()
    own_sharp.wait()
    to_scalars = pltpu.make_async_copy(adjv.at[jnp.where(same, 0, 1)], adjs, recv_small.at[1])
    to_scalars.start()
    to_scalars.wait()

    def slot_of(t):
        return lax.rem(head - t + heads, heads)

    def far_of(t):
        return adjs[NB - 1, 2 * slot_of(t) + s]

    def chain(t, _):
        mine = far_of(t)

        def look(u, found):
            return jnp.where(jnp.logical_and(u < t, far_of(u) == mine), u, found)

        prevs[t] = lax.fori_loop(0, heads, look, jnp.int32(-1))
        return _

    lax.fori_loop(0, heads, chain, None)

    def last_of(k, _):
        def look(u, found):
            return jnp.where(far_of(u) == k, u, found)

        lasts[k] = lax.fori_loop(0, heads, look, jnp.int32(-1))
        return _

    lax.fori_loop(0, chips, last_of, None)

    def clear(i, _):
        dk[0, i, :, :] = jnp.zeros((BLOCK, HD), jnp.float32)
        dk[1, i, :, :] = jnp.zeros((BLOCK, HD), jnp.float32)
        dv[0, i, :, :] = jnp.zeros((BLOCK, HD), jnp.float32)
        dv[1, i, :, :] = jnp.zeros((BLOCK, HD), jnp.float32)
        return _

    lax.fori_loop(0, heads, clear, None)

    for i, ref in enumerate((kx, vx)):
        pltpu.make_async_copy(ref.at[s], ref.at[s], recv_kv.at[i]).wait()
        to_sibling(ref.at[s], ref.at[s], send_relay.at[i], recv_relay.at[i]).start()
    for i, ref in enumerate((kx, vx)):
        pltpu.make_async_copy(ref.at[1 - s], ref.at[1 - s], recv_relay.at[i]).wait()

    sharp = sharps[head]
    scale = sharp * (1.0 / math.sqrt(HD))

    def step(t, acc):
        j = slot_of(t)
        b = 2 * j + s
        pltpu.make_async_copy(qg.at[j], qg.at[j], recv_q.at[j]).wait()
        q = qg[j, 0] * scale
        g = qg[j, 1]
        far = far_of(t)
        before = lax.rem(b + chips - 1, chips)
        after = lax.rem(b + 1, chips)

        def listed(ref):
            return jnp.concatenate(
                [ref[s, j], ref[1 - s, before // 2], ref[1 - s, after // 2], ref[far % 2, far // 2]],
                axis=0,
            )

        keys = listed(kx)
        values = listed(vx)
        logits = dot(keys, q, 1, 1)
        prob_grad = dot(values, g, 1, 1)
        top = jnp.max(logits, axis=0, keepdims=True)
        shifted = jnp.exp(logits - top)
        prob = shifted * (1.0 / jnp.sum(shifted, axis=0, keepdims=True))
        row_dot = jnp.sum(prob * prob_grad, axis=0, keepdims=True)
        score_grad = prob * (prob_grad - row_dot)
        acc = acc + jnp.sum(score_grad * logits, axis=0, keepdims=True)
        oq[j, 0] = dot(prob, values, 0, 0)
        oq[j, 1] = dot(score_grad, keys, 0, 0) * scale
        put(j, oq.at[j, 0], columns(o_ref, head), send_oq, recv_out.at[0])
        put(j, oq.at[j, 1], columns(dq_ref, head), send_oq, recv_out.at[1])
        key_terms = dot(score_grad, q, 1, 0)
        value_terms = dot(prob, g, 1, 0)
        back = prevs[t]
        at = jnp.maximum(back, 0)
        for total, run, terms in ((dk, runk, key_terms), (dv, runv, value_terms)):
            total[s, j] += terms[:BLOCK]
            total[1 - s, before // 2] += terms[BLOCK : 2 * BLOCK]
            total[1 - s, after // 2] += terms[2 * BLOCK : 3 * BLOCK]
            run[t] = terms[3 * BLOCK :] + jnp.where(back >= 0, run[at], 0.0)
        return acc

    acc = lax.fori_loop(0, heads, step, jnp.zeros((1, HD), jnp.float32))

    sh_own[...] = jnp.broadcast_to(jnp.sum(acc, axis=1, keepdims=True) / sharp, (8, HD))
    small = to_sibling(sh_own, sh_sib, send_small.at[1], recv_small.at[2])
    small.start()

    def gather(total, run, half, i):
        at = lasts[2 * i + half]
        return total[half, i] + jnp.where(at >= 0, run[jnp.maximum(at, 0)], 0.0)

    def far_sibling(i, _):
        dk[1 - s, i] = gather(dk, runk, 1 - s, i)
        dv[1 - s, i] = gather(dv, runv, 1 - s, i)
        return _

    lax.fori_loop(0, heads, far_sibling, None)
    for i, ref in enumerate((dk, dv)):
        to_sibling(ref.at[1 - s], part.at[i], send_part.at[i], recv_part.at[i]).start()

    small.wait()
    sh_tot[...] = sh_own[...] + sh_sib[...]

    def send_sharp(i, _):
        put(i, sh_tot, sh_all.at[head], send_small.at[2], recv_small.at[3])
        return _

    lax.fori_loop(0, heads, send_sharp, None)

    for i in range(2):
        pltpu.make_async_copy(part.at[i], part.at[i], recv_part.at[i]).wait()

    def finish(t, _):
        j = slot_of(t)
        dk[s, j] = gather(dk, runk, s, j) + part[0, j]
        dv[s, j] = gather(dv, runv, s, j) + part[1, j]
        put(j, dk.at[s, j], columns(dk_ref, head), send_dkv, recv_out.at[2])
        put(j, dv.at[s, j], columns(dv_ref, head), send_dkv, recv_out.at[3])
        return _

    lax.fori_loop(0, heads, finish, None)

    pltpu.make_async_copy(sh_all, sh_all, recv_small.at[3]).wait()
    dp_all[dp] = sh_all[:, 0, :]

    def send_dp(i, _):
        @pl.when(i != dp)
        def _():
            pltpu.make_async_remote_copy(
                dp_all.at[dp],
                dp_all.at[dp],
                send_small.at[3],
                recv_small.at[4],
                device_id=(i, c),
                device_id_type=MESH,
            ).start()

        return _

    lax.fori_loop(0, dps, send_dp, None)
    others = dp_all.at[pl.ds(0, dps - 1)]
    pltpu.make_async_copy(others, others, recv_small.at[4]).wait()
    total = dp_all[0]
    for i in range(1, dps):
        total = total + dp_all[i]
    lane = lax.broadcasted_iota(jnp.int32, total.shape, 1)
    row = lax.broadcasted_iota(jnp.int32, total.shape, 0)
    ds_ref[...] = jnp.sum(jnp.where(lane == row, total, 0.0), axis=0, keepdims=True)[:, :heads]

    pltpu.make_async_copy(others, others, send_small.at[3]).wait()
    for i, ref in enumerate((kx, vx)):
        pltpu.make_async_copy(ref.at[s], ref.at[s], send_relay.at[i]).wait()
    for i in range(2):
        pltpu.make_async_copy(part.at[i], part.at[i], send_part.at[i]).wait()

    def drain(count):
        few = qg.at[pl.ds(0, count)]
        pltpu.make_async_copy(few, few, send_in).wait()
        pltpu.make_async_copy(few, few, send_in).wait()
        pltpu.make_async_copy(few, few, send_oq).wait()
        pltpu.make_async_copy(few, few, send_dkv).wait()
        tiles = sh_all.at[pl.ds(0, count)]
        pltpu.make_async_copy(tiles, tiles, send_small.at[2]).wait()

    @pl.when(same)
    def _():
        drain(heads - 1)

    @pl.when(jnp.logical_not(same))
    def _():
        drain(heads)

    for i, ref in enumerate((o_ref, dq_ref, dk_ref, dv_ref)):
        pltpu.make_async_copy(ref, ref, recv_out.at[i]).wait()


def settle_kernel(*refs):
    ins, outs, sems = refs[:4], refs[4:8], refs[8]
    pieces = sems.shape[1]
    copies = []
    for a, (src, dst) in enumerate(zip(ins, outs)):
        rows = src.shape[0] // pieces
        for i in range(pieces):
            part = pl.ds(i * rows, rows)
            copies.append(pltpu.make_async_copy(src.at[part], dst.at[part], sems.at[a, i]))
    for copy in copies:
        copy.start()
    for copy in copies:
        copy.wait()


def settle(*arrays):
    anywhere = pl.BlockSpec(memory_space=pl.ANY)
    return pl.pallas_call(
        settle_kernel,
        out_shape=[jax.ShapeDtypeStruct(x.shape, x.dtype) for x in arrays],
        in_specs=[anywhere] * 4,
        out_specs=[pl.BlockSpec(memory_space=pltpu.HBM)] * 4,
        scratch_shapes=[pltpu.SemaphoreType.DMA((4, 2))],
        name="settle",
    )(*arrays)


def per_device(queries, keys, values, sharpness, listing, adjoint):
    chips = lax.axis_size("seq")
    dps = lax.axis_size("dp")
    heads = chips // 2
    rows, features = queries.shape[1:]
    f32 = jnp.float32
    anywhere = pl.BlockSpec(memory_space=pl.ANY)
    block = (BLOCK, HD)
    whole = jax.ShapeDtypeStruct((rows, features), f32)
    dma = pltpu.SemaphoreType.DMA
    o, dq, dk, dv, ds = pl.pallas_call(
        functools.partial(kernel, chips, dps),
        out_shape=[whole] * 4 + [jax.ShapeDtypeStruct((1, heads), f32)],
        in_specs=[pl.BlockSpec(memory_space=pltpu.HBM)] * 6,
        out_specs=[anywhere] * 4 + [pl.BlockSpec(memory_space=pltpu.VMEM)],
        scratch_shapes=[
            pltpu.VMEM((2, heads) + block, f32),
            pltpu.VMEM((2, heads) + block, f32),
            pltpu.VMEM((heads, 2) + block, f32),
            pltpu.VMEM((heads, 2) + block, f32),
            pltpu.VMEM((2, heads) + block, f32),
            pltpu.VMEM((2, heads) + block, f32),
            pltpu.VMEM((heads,) + block, f32),
            pltpu.VMEM((heads,) + block, f32),
            pltpu.VMEM((2, heads) + block, f32),
            pltpu.VMEM((2, NB, chips), jnp.int32),
            pltpu.SMEM((NB, chips), jnp.int32),
            pltpu.SMEM((heads,), f32),
            pltpu.SMEM((heads,), jnp.int32),
            pltpu.SMEM((chips,), jnp.int32),
            pltpu.VMEM((8, HD), f32),
            pltpu.VMEM((8, HD), f32),
            pltpu.VMEM((8, HD), f32),
            pltpu.VMEM((heads, 8, HD), f32),
            pltpu.VMEM((dps, heads, HD), f32),
            dma,
            dma((2,)),
            dma,
            dma,
            dma((2,)),
            dma((4,)),
            dma((2,)),
            dma((heads,)),
            dma((2,)),
            dma((2,)),
            dma((4,)),
            dma((6,)),
        ],
        compiler_params=pltpu.CompilerParams(
            collective_id=0, has_side_effects=True, vmem_limit_bytes=48 * 2**20
        ),
        name="attend",
    )(
        *(
            pltpu.with_memory_space_constraint(x, pltpu.HBM)
            for x in (queries[0], keys[0], values[0], adjoint[0], listing[0].T, sharpness)
        )
    )
    o, dq, dk, dv = settle(o, dq, dk, dv)
    return o[None], dq[None], dk[None], dv[None], ds[0]


def solution(mesh):
    tokens = P("dp", "seq", None)
    return jax.shard_map(
        per_device,
        mesh=mesh,
        in_specs=(tokens, tokens, tokens, P(), P("dp", None, None), tokens),
        out_specs=(tokens, tokens, tokens, tokens, P()),
        check_vma=False,
    )
```

```python
import functools
import math

import jax
import jax.numpy as jnp
from jax import lax
from jax.experimental import pallas as pl
from jax.experimental.pallas import tpu as pltpu
from jax.sharding import PartitionSpec as P

HD = 128
BLOCK = 128
NB = 4
MESH = pl.DeviceIdType.MESH
HIGH = lax.Precision.HIGHEST


def dot(a, b, ca, cb):
    return lax.dot_general(
        a, b, (((ca,), (cb,)), ((), ())), precision=HIGH, preferred_element_type=jnp.float32
    )


def kernel(
    chips,
    dps,
    q_ref,
    k_ref,
    v_ref,
    g_ref,
    adj_ref,
    sharp_ref,
    o_ref,
    dq_ref,
    dk_ref,
    dv_ref,
    ds_ref,
    kx,
    vx,
    qg,
    oq,
    dk,
    dv,
    runk,
    runv,
    part,
    adjv,
    adjs,
    sharps,
    prevs,
    lasts,
    sh_own,
    sh_sib,
    sh_tot,
    sh_all,
    dp_all,
    send_in,
    send_relay,
    send_oq,
    send_dkv,
    send_part,
    send_small,
    recv_kv,
    recv_q,
    recv_relay,
    recv_part,
    recv_out,
    recv_small,
):
    heads = chips // 2
    dp = lax.axis_index("dp")
    c = lax.axis_index("seq")
    X2 = (dp // 2) * 2
    s = dp % 2
    p = c % 2
    head = c // 2
    same = p == s
    sibling = (X2 + 1 - s, c)

    def partner(i):
        return (X2 + p, 2 * i + s)

    def is_self(i):
        return jnp.logical_and(same, 2 * i + s == c)

    barrier = pltpu.get_barrier_semaphore()

    def greet(i, _):
        @pl.when(jnp.logical_not(is_self(i)))
        def _():
            pl.semaphore_signal(barrier, inc=1, device_id=partner(i), device_id_type=MESH)

        return _

    lax.fori_loop(0, heads, greet, None)

    def greet_dp(i, _):
        @pl.when(i != dp)
        def _():
            pl.semaphore_signal(barrier, inc=1, device_id=(i, c), device_id_type=MESH)

        return _

    lax.fori_loop(0, dps, greet_dp, None)
    pl.semaphore_wait(barrier, jnp.where(same, heads - 1, heads) + dps - 1)

    def put(i, src, dst, send, recv):
        @pl.when(is_self(i))
        def _():
            pltpu.make_async_copy(src, dst, recv).start()

        @pl.when(jnp.logical_not(is_self(i)))
        def _():
            pltpu.make_async_remote_copy(
                src, dst, send, recv, device_id=partner(i), device_id_type=MESH
            ).start()

    def columns(ref, h):
        return ref.at[:, pl.ds(pl.multiple_of(h * HD, HD), HD)]

    def to_sibling(src, dst, send, recv):
        return pltpu.make_async_remote_copy(
            src, dst, send, recv, device_id=sibling, device_id_type=MESH
        )

    adj_copy = to_sibling(adj_ref, adjv.at[1], send_small.at[0], recv_small.at[0])
    adj_copy.start()
    own_adj = pltpu.make_async_copy(adj_ref, adjv.at[0], recv_small.at[1])
    own_adj.start()
    own_sharp = pltpu.make_async_copy(sharp_ref, sharps, recv_small.at[5])
    own_sharp.start()

    def send_k(t, _):
        h = lax.rem(head + t, heads)
        put(h, columns(k_ref, h), kx.at[p, head], send_in, recv_kv.at[0])
        return _

    def send_v(t, _):
        h = lax.rem(head + t, heads)
        put(h, columns(v_ref, h), vx.at[p, head], send_in, recv_kv.at[1])
        return _

    def send_q(t, _):
        h = lax.rem(head + t, heads)
        put(h, columns(q_ref, h), qg.at[head, 0], send_in, recv_q.at[head])
        put(h, columns(g_ref, h), qg.at[head, 1], send_in, recv_q.at[head])
        return _

    lax.fori_loop(0, heads, send_k, None)
    lax.fori_loop(0, heads, send_v, None)
    lax.fori_loop(0, heads, send_q, None)

    adj_copy.wait()
    own_adj.wait()
    own_sharp.wait()
    to_scalars = pltpu.make_async_copy(adjv.at[jnp.where(same, 0, 1)], adjs, recv_small.at[1])
    to_scalars.start()
    to_scalars.wait()

    def slot_of(t):
        return lax.rem(head - t + heads, heads)

    def far_of(t):
        return adjs[NB - 1, 2 * slot_of(t) + s]

    def chain(t, _):
        mine = far_of(t)

        def look(u, found):
            return jnp.where(jnp.logical_and(u < t, far_of(u) == mine), u, found)

        prevs[t] = lax.fori_loop(0, heads, look, jnp.int32(-1))
        return _

    lax.fori_loop(0, heads, chain, None)

    def last_of(k, _):
        def look(u, found):
            return jnp.where(far_of(u) == k, u, found)

        lasts[k] = lax.fori_loop(0, heads, look, jnp.int32(-1))
        return _

    lax.fori_loop(0, chips, last_of, None)

    def clear(i, _):
        dk[0, i, :, :] = jnp.zeros((BLOCK, HD), jnp.float32)
        dk[1, i, :, :] = jnp.zeros((BLOCK, HD), jnp.float32)
        dv[0, i, :, :] = jnp.zeros((BLOCK, HD), jnp.float32)
        dv[1, i, :, :] = jnp.zeros((BLOCK, HD), jnp.float32)
        return _

    lax.fori_loop(0, heads, clear, None)

    for i, ref in enumerate((kx, vx)):
        pltpu.make_async_copy(ref.at[s], ref.at[s], recv_kv.at[i]).wait()
        to_sibling(ref.at[s], ref.at[s], send_relay.at[i], recv_relay.at[i]).start()
    for i, ref in enumerate((kx, vx)):
        pltpu.make_async_copy(ref.at[1 - s], ref.at[1 - s], recv_relay.at[i]).wait()

    sharp = sharps[head]
    scale = sharp * (1.0 / math.sqrt(HD))

    def step(t, acc):
        j = slot_of(t)
        b = 2 * j + s
        pltpu.make_async_copy(qg.at[j], qg.at[j], recv_q.at[j]).wait()
        q = qg[j, 0] * scale
        g = qg[j, 1]
        far = far_of(t)
        before = lax.rem(b + chips - 1, chips)
        after = lax.rem(b + 1, chips)

        def listed(ref):
            return jnp.concatenate(
                [ref[s, j], ref[1 - s, before // 2], ref[1 - s, after // 2], ref[far % 2, far // 2]],
                axis=0,
            )

        keys = listed(kx)
        values = listed(vx)
        logits = dot(keys, q, 1, 1)
        prob_grad = dot(values, g, 1, 1)
        top = jnp.max(logits, axis=0, keepdims=True)
        shifted = jnp.exp(logits - top)
        prob = shifted * (1.0 / jnp.sum(shifted, axis=0, keepdims=True))
        row_dot = jnp.sum(prob * prob_grad, axis=0, keepdims=True)
        score_grad = prob * (prob_grad - row_dot)
        acc = acc + jnp.sum(score_grad * logits, axis=0, keepdims=True)
        oq[j, 0] = dot(prob, values, 0, 0)
        oq[j, 1] = dot(score_grad, keys, 0, 0) * scale
        put(j, oq.at[j, 0], columns(o_ref, head), send_oq, recv_out.at[0])
        put(j, oq.at[j, 1], columns(dq_ref, head), send_oq, recv_out.at[1])
        key_terms = dot(score_grad, q, 1, 0)
        value_terms = dot(prob, g, 1, 0)
        back = prevs[t]
        at = jnp.maximum(back, 0)
        for total, run, terms in ((dk, runk, key_terms), (dv, runv, value_terms)):
            total[s, j] += terms[:BLOCK]
            total[1 - s, before // 2] += terms[BLOCK : 2 * BLOCK]
            total[1 - s, after // 2] += terms[2 * BLOCK : 3 * BLOCK]
            run[t] = terms[3 * BLOCK :] + jnp.where(back >= 0, run[at], 0.0)
        return acc

    acc = lax.fori_loop(0, heads, step, jnp.zeros((1, HD), jnp.float32))

    sh_own[...] = jnp.broadcast_to(jnp.sum(acc, axis=1, keepdims=True) / sharp, (8, HD))
    small = to_sibling(sh_own, sh_sib, send_small.at[1], recv_small.at[2])
    small.start()

    def gather(total, run, half, i):
        at = lasts[2 * i + half]
        return total[half, i] + jnp.where(at >= 0, run[jnp.maximum(at, 0)], 0.0)

    def far_sibling(i, _):
        dk[1 - s, i] = gather(dk, runk, 1 - s, i)
        dv[1 - s, i] = gather(dv, runv, 1 - s, i)
        return _

    lax.fori_loop(0, heads, far_sibling, None)
    for i, ref in enumerate((dk, dv)):
        to_sibling(ref.at[1 - s], part.at[i], send_part.at[i], recv_part.at[i]).start()

    small.wait()
    sh_tot[...] = sh_own[...] + sh_sib[...]

    def send_sharp(i, _):
        put(i, sh_tot, sh_all.at[head], send_small.at[2], recv_small.at[3])
        return _

    lax.fori_loop(0, heads, send_sharp, None)

    for i in range(2):
        pltpu.make_async_copy(part.at[i], part.at[i], recv_part.at[i]).wait()

    def finish(t, _):
        j = slot_of(t)
        dk[s, j] = gather(dk, runk, s, j) + part[0, j]
        dv[s, j] = gather(dv, runv, s, j) + part[1, j]
        put(j, dk.at[s, j], columns(dk_ref, head), send_dkv, recv_out.at[2])
        put(j, dv.at[s, j], columns(dv_ref, head), send_dkv, recv_out.at[3])
        return _

    lax.fori_loop(0, heads, finish, None)

    pltpu.make_async_copy(sh_all, sh_all, recv_small.at[3]).wait()
    dp_all[dp] = sh_all[:, 0, :]

    def send_dp(i, _):
        @pl.when(i != dp)
        def _():
            pltpu.make_async_remote_copy(
                dp_all.at[dp],
                dp_all.at[dp],
                send_small.at[3],
                recv_small.at[4],
                device_id=(i, c),
                device_id_type=MESH,
            ).start()

        return _

    lax.fori_loop(0, dps, send_dp, None)
    others = dp_all.at[pl.ds(0, dps - 1)]
    pltpu.make_async_copy(others, others, recv_small.at[4]).wait()
    total = dp_all[0]
    for i in range(1, dps):
        total = total + dp_all[i]
    lane = lax.broadcasted_iota(jnp.int32, total.shape, 1)
    row = lax.broadcasted_iota(jnp.int32, total.shape, 0)
    ds_ref[...] = jnp.sum(jnp.where(lane == row, total, 0.0), axis=0, keepdims=True)[:, :heads]

    pltpu.make_async_copy(others, others, send_small.at[3]).wait()
    for i, ref in enumerate((kx, vx)):
        pltpu.make_async_copy(ref.at[s], ref.at[s], send_relay.at[i]).wait()
    for i in range(2):
        pltpu.make_async_copy(part.at[i], part.at[i], send_part.at[i]).wait()

    def drain(count):
        few = qg.at[pl.ds(0, count)]
        pltpu.make_async_copy(few, few, send_in).wait()
        pltpu.make_async_copy(few, few, send_in).wait()
        pltpu.make_async_copy(few, few, send_oq).wait()
        pltpu.make_async_copy(few, few, send_dkv).wait()
        tiles = sh_all.at[pl.ds(0, count)]
        pltpu.make_async_copy(tiles, tiles, send_small.at[2]).wait()

    @pl.when(same)
    def _():
        drain(heads - 1)

    @pl.when(jnp.logical_not(same))
    def _():
        drain(heads)

    for i, ref in enumerate((o_ref, dq_ref, dk_ref, dv_ref)):
        pltpu.make_async_copy(ref, ref, recv_out.at[i]).wait()


def settle_kernel(*refs):
    ins, outs, sems, last = refs[:5], refs[5:10], refs[10], refs[11]
    pieces = sems.shape[1]
    copies = [pltpu.make_async_copy(ins[4], outs[4], last)]
    for a, (src, dst) in enumerate(zip(ins[:4], outs[:4])):
        rows = src.shape[0] // pieces
        for i in range(pieces):
            part = pl.ds(i * rows, rows)
            copies.append(pltpu.make_async_copy(src.at[part], dst.at[part], sems.at[a, i]))
    for copy in copies:
        copy.start()
    for copy in copies:
        copy.wait()


def settle(*arrays):
    return pl.pallas_call(
        settle_kernel,
        out_shape=[jax.ShapeDtypeStruct(x.shape, x.dtype) for x in arrays],
        in_specs=[pl.BlockSpec(memory_space=pltpu.VMEM)] * 5,
        out_specs=[pl.BlockSpec(memory_space=pltpu.HBM)] * 5,
        scratch_shapes=[pltpu.SemaphoreType.DMA((4, 2)), pltpu.SemaphoreType.DMA],
        compiler_params=pltpu.CompilerParams(vmem_limit_bytes=6 * 2**20),
        name="settle",
    )(*arrays)


def per_device(queries, keys, values, sharpness, listing, adjoint):
    chips = lax.axis_size("seq")
    dps = lax.axis_size("dp")
    heads = chips // 2
    rows, features = queries.shape[1:]
    f32 = jnp.float32
    anywhere = pl.BlockSpec(memory_space=pl.ANY)
    block = (BLOCK, HD)
    whole = jax.ShapeDtypeStruct((rows, features), f32)
    dma = pltpu.SemaphoreType.DMA
    o, dq, dk, dv, ds = pl.pallas_call(
        functools.partial(kernel, chips, dps),
        out_shape=[whole] * 4 + [jax.ShapeDtypeStruct((1, heads), f32)],
        in_specs=[pl.BlockSpec(memory_space=pltpu.HBM)] * 6,
        out_specs=[anywhere] * 4 + [pl.BlockSpec(memory_space=pltpu.VMEM)],
        scratch_shapes=[
            pltpu.VMEM((2, heads) + block, f32),
            pltpu.VMEM((2, heads) + block, f32),
            pltpu.VMEM((heads, 2) + block, f32),
            pltpu.VMEM((heads, 2) + block, f32),
            pltpu.VMEM((2, heads) + block, f32),
            pltpu.VMEM((2, heads) + block, f32),
            pltpu.VMEM((heads,) + block, f32),
            pltpu.VMEM((heads,) + block, f32),
            pltpu.VMEM((2, heads) + block, f32),
            pltpu.VMEM((2, NB, chips), jnp.int32),
            pltpu.SMEM((NB, chips), jnp.int32),
            pltpu.SMEM((heads,), f32),
            pltpu.SMEM((heads,), jnp.int32),
            pltpu.SMEM((chips,), jnp.int32),
            pltpu.VMEM((8, HD), f32),
            pltpu.VMEM((8, HD), f32),
            pltpu.VMEM((8, HD), f32),
            pltpu.VMEM((heads, 8, HD), f32),
            pltpu.VMEM((dps, heads, HD), f32),
            dma,
            dma((2,)),
            dma,
            dma,
            dma((2,)),
            dma((4,)),
            dma((2,)),
            dma((heads,)),
            dma((2,)),
            dma((2,)),
            dma((4,)),
            dma((6,)),
        ],
        compiler_params=pltpu.CompilerParams(
            collective_id=0, has_side_effects=True, vmem_limit_bytes=48 * 2**20
        ),
        name="attend",
    )(
        *(
            pltpu.with_memory_space_constraint(x, pltpu.HBM)
            for x in (queries[0], keys[0], values[0], adjoint[0], listing[0].T, sharpness)
        )
    )
    o, dq, dk, dv, ds = settle(o, dq, dk, dv, ds)
    return o[None], dq[None], dk[None], dv[None], ds[0]


def solution(mesh):
    tokens = P("dp", "seq", None)
    return jax.shard_map(
        per_device,
        mesh=mesh,
        in_specs=(tokens, tokens, tokens, P(), P("dp", None, None), tokens),
        out_specs=(tokens, tokens, tokens, tokens, P()),
        check_vma=False,
    )
```

```python
import functools
import math

import jax
import jax.numpy as jnp
from jax import lax
from jax.experimental import pallas as pl
from jax.experimental.pallas import tpu as pltpu
from jax.sharding import PartitionSpec as P

HD = 128
BLOCK = 128
NB = 4
MESH = pl.DeviceIdType.MESH
HIGH = lax.Precision.HIGHEST


def dot(a, b, ca, cb):
    return lax.dot_general(
        a, b, (((ca,), (cb,)), ((), ())), precision=HIGH, preferred_element_type=jnp.float32
    )


def kernel(
    chips,
    dps,
    q_ref,
    k_ref,
    v_ref,
    g_ref,
    adj_ref,
    sharp_ref,
    o_ref,
    dq_ref,
    dk_ref,
    dv_ref,
    ds_ref,
    kx,
    vx,
    qg,
    oq,
    dk,
    dv,
    runk,
    runv,
    part,
    adjv,
    adjs,
    sharps,
    prevs,
    lasts,
    sh_own,
    sh_sib,
    sh_tot,
    sh_all,
    dp_all,
    send_in,
    send_relay,
    send_oq,
    send_dkv,
    send_part,
    send_small,
    recv_kv,
    recv_q,
    recv_relay,
    recv_part,
    recv_out,
    recv_small,
):
    heads = chips // 2
    dp = lax.axis_index("dp")
    c = lax.axis_index("seq")
    X2 = (dp // 2) * 2
    s = dp % 2
    p = c % 2
    head = c // 2
    same = p == s
    sibling = (X2 + 1 - s, c)

    def partner(i):
        return (X2 + p, 2 * i + s)

    def is_self(i):
        return jnp.logical_and(same, 2 * i + s == c)

    barrier = pltpu.get_barrier_semaphore()

    def greet(i, _):
        @pl.when(jnp.logical_not(is_self(i)))
        def _():
            pl.semaphore_signal(barrier, inc=1, device_id=partner(i), device_id_type=MESH)

        return _

    lax.fori_loop(0, heads, greet, None)

    def greet_dp(i, _):
        @pl.when(i != dp)
        def _():
            pl.semaphore_signal(barrier, inc=1, device_id=(i, c), device_id_type=MESH)

        return _

    lax.fori_loop(0, dps, greet_dp, None)
    pl.semaphore_wait(barrier, jnp.where(same, heads - 1, heads) + dps - 1)

    def put(i, src, dst, send, recv):
        @pl.when(is_self(i))
        def _():
            pltpu.make_async_copy(src, dst, recv).start()

        @pl.when(jnp.logical_not(is_self(i)))
        def _():
            pltpu.make_async_remote_copy(
                src, dst, send, recv, device_id=partner(i), device_id_type=MESH
            ).start()

    def columns(ref, h):
        return ref.at[:, pl.ds(pl.multiple_of(h * HD, HD), HD)]

    def to_sibling(src, dst, send, recv):
        return pltpu.make_async_remote_copy(
            src, dst, send, recv, device_id=sibling, device_id_type=MESH
        )

    adj_copy = to_sibling(adj_ref, adjv.at[1], send_small.at[0], recv_small.at[0])
    adj_copy.start()
    own_adj = pltpu.make_async_copy(adj_ref, adjv.at[0], recv_small.at[1])
    own_adj.start()
    own_sharp = pltpu.make_async_copy(sharp_ref, sharps, recv_small.at[5])
    own_sharp.start()

    def send_k(t, _):
        h = lax.rem(head + t, heads)
        put(h, columns(k_ref, h), kx.at[p, head], send_in, recv_kv.at[0])
        return _

    def send_v(t, _):
        h = lax.rem(head + t, heads)
        put(h, columns(v_ref, h), vx.at[p, head], send_in, recv_kv.at[1])
        return _

    def send_q(t, _):
        h = lax.rem(head + t, heads)
        put(h, columns(q_ref, h), qg.at[head, 0], send_in, recv_q.at[head])
        put(h, columns(g_ref, h), qg.at[head, 1], send_in, recv_q.at[head])
        return _

    lax.fori_loop(0, heads, send_k, None)
    lax.fori_loop(0, heads, send_v, None)
    lax.fori_loop(0, heads, send_q, None)

    adj_copy.wait()
    own_adj.wait()
    own_sharp.wait()
    to_scalars = pltpu.make_async_copy(adjv.at[jnp.where(same, 0, 1)], adjs, recv_small.at[1])
    to_scalars.start()
    to_scalars.wait()

    def slot_of(t):
        return lax.rem(head - t + heads, heads)

    def far_of(t):
        return adjs[NB - 1, 2 * slot_of(t) + s]

    def chain(t, _):
        mine = far_of(t)

        def look(u, found):
            return jnp.where(jnp.logical_and(u < t, far_of(u) == mine), u, found)

        prevs[t] = lax.fori_loop(0, heads, look, jnp.int32(-1))
        return _

    lax.fori_loop(0, heads, chain, None)

    def last_of(k, _):
        def look(u, found):
            return jnp.where(far_of(u) == k, u, found)

        lasts[k] = lax.fori_loop(0, heads, look, jnp.int32(-1))
        return _

    lax.fori_loop(0, chips, last_of, None)

    def clear(i, _):
        dk[0, i, :, :] = jnp.zeros((BLOCK, HD), jnp.float32)
        dk[1, i, :, :] = jnp.zeros((BLOCK, HD), jnp.float32)
        dv[0, i, :, :] = jnp.zeros((BLOCK, HD), jnp.float32)
        dv[1, i, :, :] = jnp.zeros((BLOCK, HD), jnp.float32)
        return _

    lax.fori_loop(0, heads, clear, None)

    for i, ref in enumerate((kx, vx)):
        pltpu.make_async_copy(ref.at[s], ref.at[s], recv_kv.at[i]).wait()
        to_sibling(ref.at[s], ref.at[s], send_relay.at[i], recv_relay.at[i]).start()
    for i, ref in enumerate((kx, vx)):
        pltpu.make_async_copy(ref.at[1 - s], ref.at[1 - s], recv_relay.at[i]).wait()

    sharp = sharps[head]
    scale = sharp * (1.0 / math.sqrt(HD))

    def step(t, acc):
        j = slot_of(t)
        b = 2 * j + s
        pltpu.make_async_copy(qg.at[j], qg.at[j], recv_q.at[j]).wait()
        q = qg[j, 0] * scale
        g = qg[j, 1]
        far = far_of(t)
        before = lax.rem(b + chips - 1, chips)
        after = lax.rem(b + 1, chips)

        def listed(ref):
            return jnp.concatenate(
                [ref[s, j], ref[1 - s, before // 2], ref[1 - s, after // 2], ref[far % 2, far // 2]],
                axis=0,
            )

        keys = listed(kx)
        values = listed(vx)
        logits = dot(keys, q, 1, 1)
        prob_grad = dot(values, g, 1, 1)
        top = jnp.max(logits, axis=0, keepdims=True)
        shifted = jnp.exp(logits - top)
        prob = shifted * (1.0 / jnp.sum(shifted, axis=0, keepdims=True))
        row_dot = jnp.sum(prob * prob_grad, axis=0, keepdims=True)
        score_grad = prob * (prob_grad - row_dot)
        acc = acc + jnp.sum(score_grad * logits, axis=0, keepdims=True)
        oq[j, 0] = dot(prob, values, 0, 0)
        oq[j, 1] = dot(score_grad, keys, 0, 0) * scale
        put(j, oq.at[j, 0], columns(o_ref, head), send_oq, recv_out.at[0])
        put(j, oq.at[j, 1], columns(dq_ref, head), send_oq, recv_out.at[1])
        key_terms = dot(score_grad, q, 1, 0)
        value_terms = dot(prob, g, 1, 0)
        back = prevs[t]
        at = jnp.maximum(back, 0)
        for total, run, terms in ((dk, runk, key_terms), (dv, runv, value_terms)):
            total[s, j] += terms[:BLOCK]
            total[1 - s, before // 2] += terms[BLOCK : 2 * BLOCK]
            total[1 - s, after // 2] += terms[2 * BLOCK : 3 * BLOCK]
            run[t] = terms[3 * BLOCK :] + jnp.where(back >= 0, run[at], 0.0)
        return acc

    acc = lax.fori_loop(0, heads, step, jnp.zeros((1, HD), jnp.float32))

    sh_own[...] = jnp.broadcast_to(jnp.sum(acc, axis=1, keepdims=True) / sharp, (8, HD))
    small = to_sibling(sh_own, sh_sib, send_small.at[1], recv_small.at[2])
    small.start()

    def gather(total, run, half, i):
        at = lasts[2 * i + half]
        return total[half, i] + jnp.where(at >= 0, run[jnp.maximum(at, 0)], 0.0)

    def far_sibling(i, _):
        dk[1 - s, i] = gather(dk, runk, 1 - s, i)
        dv[1 - s, i] = gather(dv, runv, 1 - s, i)
        return _

    lax.fori_loop(0, heads, far_sibling, None)
    for i, ref in enumerate((dk, dv)):
        to_sibling(ref.at[1 - s], part.at[i], send_part.at[i], recv_part.at[i]).start()

    small.wait()
    sh_tot[...] = sh_own[...] + sh_sib[...]

    def send_sharp(i, _):
        put(i, sh_tot, sh_all.at[head], send_small.at[2], recv_small.at[3])
        return _

    lax.fori_loop(0, heads, send_sharp, None)

    for i in range(2):
        pltpu.make_async_copy(part.at[i], part.at[i], recv_part.at[i]).wait()

    def order(t):
        i = t // 4
        r = t % 4
        return jnp.where(r == 0, (4 * i + 2), jnp.where(r == 1, 4 * i + 1, jnp.where(r == 2, (4 * i + 8) % 16, 4 * i + 3)))

    def finish_k(t, _):
        j = slot_of(order(t))
        dk[s, j] = gather(dk, runk, s, j) + part[0, j]
        put(j, dk.at[s, j], columns(dk_ref, head), send_dkv, recv_out.at[2])
        return _

    def finish_v(t, _):
        j = slot_of(order(t))
        dv[s, j] = gather(dv, runv, s, j) + part[1, j]
        put(j, dv.at[s, j], columns(dv_ref, head), send_dkv, recv_out.at[3])
        return _

    lax.fori_loop(0, heads, finish_k, None)
    lax.fori_loop(0, heads, finish_v, None)

    pltpu.make_async_copy(sh_all, sh_all, recv_small.at[3]).wait()
    dp_all[dp] = sh_all[:, 0, :]

    def send_dp(i, _):
        @pl.when(i != dp)
        def _():
            pltpu.make_async_remote_copy(
                dp_all.at[dp],
                dp_all.at[dp],
                send_small.at[3],
                recv_small.at[4],
                device_id=(i, c),
                device_id_type=MESH,
            ).start()

        return _

    lax.fori_loop(0, dps, send_dp, None)
    others = dp_all.at[pl.ds(0, dps - 1)]
    pltpu.make_async_copy(others, others, recv_small.at[4]).wait()
    total = dp_all[0]
    for i in range(1, dps):
        total = total + dp_all[i]
    lane = lax.broadcasted_iota(jnp.int32, total.shape, 1)
    row = lax.broadcasted_iota(jnp.int32, total.shape, 0)
    ds_ref[...] = jnp.sum(jnp.where(lane == row, total, 0.0), axis=0, keepdims=True)[:, :heads]

    pltpu.make_async_copy(others, others, send_small.at[3]).wait()
    for i, ref in enumerate((kx, vx)):
        pltpu.make_async_copy(ref.at[s], ref.at[s], send_relay.at[i]).wait()
    for i in range(2):
        pltpu.make_async_copy(part.at[i], part.at[i], send_part.at[i]).wait()

    def drain(count):
        few = qg.at[pl.ds(0, count)]
        pltpu.make_async_copy(few, few, send_in).wait()
        pltpu.make_async_copy(few, few, send_in).wait()
        pltpu.make_async_copy(few, few, send_oq).wait()
        pltpu.make_async_copy(few, few, send_dkv).wait()
        tiles = sh_all.at[pl.ds(0, count)]
        pltpu.make_async_copy(tiles, tiles, send_small.at[2]).wait()

    @pl.when(same)
    def _():
        drain(heads - 1)

    @pl.when(jnp.logical_not(same))
    def _():
        drain(heads)

    for i, ref in enumerate((o_ref, dq_ref, dk_ref, dv_ref)):
        pltpu.make_async_copy(ref, ref, recv_out.at[i]).wait()


def settle_kernel(*refs):
    ins, outs, sems, last = refs[:5], refs[5:10], refs[10], refs[11]
    pieces = sems.shape[1]
    copies = [pltpu.make_async_copy(ins[4], outs[4], last)]
    for a, (src, dst) in enumerate(zip(ins[:4], outs[:4])):
        rows = src.shape[0] // pieces
        for i in range(pieces):
            part = pl.ds(i * rows, rows)
            copies.append(pltpu.make_async_copy(src.at[part], dst.at[part], sems.at[a, i]))
    for copy in copies:
        copy.start()
    for copy in copies:
        copy.wait()


def settle(*arrays):
    return pl.pallas_call(
        settle_kernel,
        out_shape=[jax.ShapeDtypeStruct(x.shape, x.dtype) for x in arrays],
        in_specs=[pl.BlockSpec(memory_space=pltpu.VMEM)] * 5,
        out_specs=[pl.BlockSpec(memory_space=pltpu.HBM)] * 5,
        scratch_shapes=[pltpu.SemaphoreType.DMA((4, 2)), pltpu.SemaphoreType.DMA],
        compiler_params=pltpu.CompilerParams(vmem_limit_bytes=6 * 2**20),
        name="settle",
    )(*arrays)


def per_device(queries, keys, values, sharpness, listing, adjoint):
    chips = lax.axis_size("seq")
    dps = lax.axis_size("dp")
    heads = chips // 2
    rows, features = queries.shape[1:]
    f32 = jnp.float32
    anywhere = pl.BlockSpec(memory_space=pl.ANY)
    block = (BLOCK, HD)
    whole = jax.ShapeDtypeStruct((rows, features), f32)
    dma = pltpu.SemaphoreType.DMA
    o, dq, dk, dv, ds = pl.pallas_call(
        functools.partial(kernel, chips, dps),
        out_shape=[whole] * 4 + [jax.ShapeDtypeStruct((1, heads), f32)],
        in_specs=[pl.BlockSpec(memory_space=pltpu.HBM)] * 6,
        out_specs=[anywhere] * 4 + [pl.BlockSpec(memory_space=pltpu.VMEM)],
        scratch_shapes=[
            pltpu.VMEM((2, heads) + block, f32),
            pltpu.VMEM((2, heads) + block, f32),
            pltpu.VMEM((heads, 2) + block, f32),
            pltpu.VMEM((heads, 2) + block, f32),
            pltpu.VMEM((2, heads) + block, f32),
            pltpu.VMEM((2, heads) + block, f32),
            pltpu.VMEM((heads,) + block, f32),
            pltpu.VMEM((heads,) + block, f32),
            pltpu.VMEM((2, heads) + block, f32),
            pltpu.VMEM((2, NB, chips), jnp.int32),
            pltpu.SMEM((NB, chips), jnp.int32),
            pltpu.SMEM((heads,), f32),
            pltpu.SMEM((heads,), jnp.int32),
            pltpu.SMEM((chips,), jnp.int32),
            pltpu.VMEM((8, HD), f32),
            pltpu.VMEM((8, HD), f32),
            pltpu.VMEM((8, HD), f32),
            pltpu.VMEM((heads, 8, HD), f32),
            pltpu.VMEM((dps, heads, HD), f32),
            dma,
            dma((2,)),
            dma,
            dma,
            dma((2,)),
            dma((4,)),
            dma((2,)),
            dma((heads,)),
            dma((2,)),
            dma((2,)),
            dma((4,)),
            dma((6,)),
        ],
        compiler_params=pltpu.CompilerParams(
            collective_id=0, has_side_effects=True, vmem_limit_bytes=48 * 2**20
        ),
        name="attend",
    )(
        *(
            pltpu.with_memory_space_constraint(x, pltpu.HBM)
            for x in (queries[0], keys[0], values[0], adjoint[0], listing[0].T, sharpness)
        )
    )
    o, dq, dk, dv, ds = settle(o, dq, dk, dv, ds)
    return o[None], dq[None], dk[None], dv[None], ds[0]


def solution(mesh):
    tokens = P("dp", "seq", None)
    return jax.shard_map(
        per_device,
        mesh=mesh,
        in_specs=(tokens, tokens, tokens, P(), P("dp", None, None), tokens),
        out_specs=(tokens, tokens, tokens, tokens, P()),
        check_vma=False,
    )
```

```python
import functools
import math

import jax
import jax.numpy as jnp
from jax import lax
from jax.experimental import pallas as pl
from jax.experimental.pallas import tpu as pltpu
from jax.sharding import PartitionSpec as P

HD = 128
BLOCK = 128
NB = 4
MESH = pl.DeviceIdType.MESH
HIGH = lax.Precision.HIGHEST


def dot(a, b, ca, cb):
    return lax.dot_general(
        a, b, (((ca,), (cb,)), ((), ())), precision=HIGH, preferred_element_type=jnp.float32
    )


def kernel(
    chips,
    dps,
    q_ref,
    k_ref,
    v_ref,
    g_ref,
    adj_ref,
    sharp_ref,
    o_ref,
    dq_ref,
    dk_ref,
    dv_ref,
    ds_ref,
    kx,
    vx,
    qg,
    oq,
    dk,
    dv,
    runk,
    runv,
    part,
    adjv,
    adjs,
    sharps,
    prevs,
    lasts,
    sh_own,
    sh_sib,
    sh_tot,
    sh_all,
    dp_all,
    send_in,
    send_relay,
    send_oq,
    send_dkv,
    send_part,
    send_small,
    recv_kv,
    recv_q,
    recv_relay,
    recv_part,
    recv_out,
    recv_small,
):
    heads = chips // 2
    dp = lax.axis_index("dp")
    c = lax.axis_index("seq")
    X2 = (dp // 2) * 2
    s = dp % 2
    p = c % 2
    head = c // 2
    same = p == s
    sibling = (X2 + 1 - s, c)

    def partner(i):
        return (X2 + p, 2 * i + s)

    def is_self(i):
        return jnp.logical_and(same, 2 * i + s == c)

    barrier = pltpu.get_barrier_semaphore()

    def greet(i, _):
        @pl.when(jnp.logical_not(is_self(i)))
        def _():
            pl.semaphore_signal(barrier, inc=1, device_id=partner(i), device_id_type=MESH)

        return _

    lax.fori_loop(0, heads, greet, None)

    def greet_dp(i, _):
        @pl.when(i != dp)
        def _():
            pl.semaphore_signal(barrier, inc=1, device_id=(i, c), device_id_type=MESH)

        return _

    lax.fori_loop(0, dps, greet_dp, None)
    pl.semaphore_wait(barrier, jnp.where(same, heads - 1, heads) + dps - 1)

    def put(i, src, dst, send, recv):
        @pl.when(is_self(i))
        def _():
            pltpu.make_async_copy(src, dst, recv).start()

        @pl.when(jnp.logical_not(is_self(i)))
        def _():
            pltpu.make_async_remote_copy(
                src, dst, send, recv, device_id=partner(i), device_id_type=MESH
            ).start()

    def columns(ref, h):
        return ref.at[:, pl.ds(pl.multiple_of(h * HD, HD), HD)]

    def to_sibling(src, dst, send, recv):
        return pltpu.make_async_remote_copy(
            src, dst, send, recv, device_id=sibling, device_id_type=MESH
        )

    adj_copy = to_sibling(adj_ref, adjv.at[1], send_small.at[0], recv_small.at[0])
    adj_copy.start()
    own_adj = pltpu.make_async_copy(adj_ref, adjv.at[0], recv_small.at[1])
    own_adj.start()
    own_sharp = pltpu.make_async_copy(sharp_ref, sharps, recv_small.at[5])
    own_sharp.start()

    def send_k(t, _):
        h = lax.rem(head + t, heads)
        put(h, columns(k_ref, h), kx.at[p, head], send_in, recv_kv.at[0])
        return _

    def send_v(t, _):
        h = lax.rem(head + t, heads)
        put(h, columns(v_ref, h), vx.at[p, head], send_in, recv_kv.at[1])
        return _

    def send_q(t, _):
        h = lax.rem(head + t, heads)
        put(h, columns(q_ref, h), qg.at[head, 0], send_in, recv_q.at[head])
        put(h, columns(g_ref, h), qg.at[head, 1], send_in, recv_q.at[head])
        return _

    lax.fori_loop(0, heads, send_k, None)
    lax.fori_loop(0, heads, send_v, None)
    lax.fori_loop(0, heads, send_q, None)

    adj_copy.wait()
    own_adj.wait()
    own_sharp.wait()
    to_scalars = pltpu.make_async_copy(adjv.at[jnp.where(same, 0, 1)], adjs, recv_small.at[1])
    to_scalars.start()
    to_scalars.wait()

    def slot_of(t):
        return lax.rem(head - t + heads, heads)

    def far_of(t):
        return adjs[NB - 1, 2 * slot_of(t) + s]

    def chain(t, _):
        mine = far_of(t)

        def look(u, found):
            return jnp.where(jnp.logical_and(u < t, far_of(u) == mine), u, found)

        prevs[t] = lax.fori_loop(0, heads, look, jnp.int32(-1))
        return _

    lax.fori_loop(0, heads, chain, None)

    def last_of(k, _):
        def look(u, found):
            return jnp.where(far_of(u) == k, u, found)

        lasts[k] = lax.fori_loop(0, heads, look, jnp.int32(-1))
        return _

    lax.fori_loop(0, chips, last_of, None)

    def clear(i, _):
        dk[0, i, :, :] = jnp.zeros((BLOCK, HD), jnp.float32)
        dk[1, i, :, :] = jnp.zeros((BLOCK, HD), jnp.float32)
        dv[0, i, :, :] = jnp.zeros((BLOCK, HD), jnp.float32)
        dv[1, i, :, :] = jnp.zeros((BLOCK, HD), jnp.float32)
        return _

    lax.fori_loop(0, heads, clear, None)

    for i, ref in enumerate((kx, vx)):
        pltpu.make_async_copy(ref.at[s], ref.at[s], recv_kv.at[i]).wait()
        to_sibling(ref.at[s], ref.at[s], send_relay.at[i], recv_relay.at[i]).start()
    for i, ref in enumerate((kx, vx)):
        pltpu.make_async_copy(ref.at[1 - s], ref.at[1 - s], recv_relay.at[i]).wait()

    sharp = sharps[head]
    scale = sharp * (1.0 / math.sqrt(HD))

    def step(t, acc):
        j = slot_of(t)
        b = 2 * j + s
        pltpu.make_async_copy(qg.at[j], qg.at[j], recv_q.at[j]).wait()
        q = qg[j, 0] * scale
        g = qg[j, 1]
        far = far_of(t)
        before = lax.rem(b + chips - 1, chips)
        after = lax.rem(b + 1, chips)

        def listed(ref):
            return jnp.concatenate(
                [ref[s, j], ref[1 - s, before // 2], ref[1 - s, after // 2], ref[far % 2, far // 2]],
                axis=0,
            )

        keys = listed(kx)
        values = listed(vx)
        logits = dot(keys, q, 1, 1)
        prob_grad = dot(values, g, 1, 1)
        top = jnp.max(logits, axis=0, keepdims=True)
        shifted = jnp.exp(logits - top)
        prob = shifted * (1.0 / jnp.sum(shifted, axis=0, keepdims=True))
        row_dot = jnp.sum(prob * prob_grad, axis=0, keepdims=True)
        score_grad = prob * (prob_grad - row_dot)
        acc = acc + jnp.sum(score_grad * logits, axis=0, keepdims=True)
        oq[j, 0] = dot(prob, values, 0, 0)
        oq[j, 1] = dot(score_grad, keys, 0, 0) * scale
        put(j, oq.at[j, 0], columns(o_ref, head), send_oq, recv_out.at[0])
        put(j, oq.at[j, 1], columns(dq_ref, head), send_oq, recv_out.at[1])
        key_terms = dot(score_grad, q, 1, 0)
        value_terms = dot(prob, g, 1, 0)
        back = prevs[t]
        at = jnp.maximum(back, 0)
        for total, run, terms in ((dk, runk, key_terms), (dv, runv, value_terms)):
            total[s, j] += terms[:BLOCK]
            total[1 - s, before // 2] += terms[BLOCK : 2 * BLOCK]
            total[1 - s, after // 2] += terms[2 * BLOCK : 3 * BLOCK]
            run[t] = terms[3 * BLOCK :] + jnp.where(back >= 0, run[at], 0.0)
        return acc

    acc = lax.fori_loop(0, heads, step, jnp.zeros((1, HD), jnp.float32))

    sh_own[...] = jnp.broadcast_to(jnp.sum(acc, axis=1, keepdims=True) / sharp, (8, HD))
    small = to_sibling(sh_own, sh_sib, send_small.at[1], recv_small.at[2])
    small.start()

    def gather(total, run, half, i):
        at = lasts[2 * i + half]
        return total[half, i] + jnp.where(at >= 0, run[jnp.maximum(at, 0)], 0.0)

    for a, (total, run) in enumerate(((dk, runk), (dv, runv))):

        def far_sibling(i, _, total=total, run=run):
            total[1 - s, i] = gather(total, run, 1 - s, i)
            return _

        lax.fori_loop(0, heads, far_sibling, None)
        to_sibling(total.at[1 - s], part.at[a], send_part.at[a], recv_part.at[a]).start()

    small.wait()
    sh_tot[...] = sh_own[...] + sh_sib[...]

    def send_sharp(i, _):
        put(i, sh_tot, sh_all.at[head], send_small.at[2], recv_small.at[3])
        return _

    lax.fori_loop(0, heads, send_sharp, None)

    def order(t):
        i = t // 4
        r = t % 4
        return jnp.where(r == 0, (4 * i + 2), jnp.where(r == 1, 4 * i + 1, jnp.where(r == 2, (4 * i + 8) % 16, 4 * i + 3)))

    def finish_k(t, _):
        j = slot_of(order(t))
        dk[s, j] = gather(dk, runk, s, j) + part[0, j]
        put(j, dk.at[s, j], columns(dk_ref, head), send_dkv, recv_out.at[2])
        return _

    def finish_v(t, _):
        j = slot_of(order(t))
        dv[s, j] = gather(dv, runv, s, j) + part[1, j]
        put(j, dv.at[s, j], columns(dv_ref, head), send_dkv, recv_out.at[3])
        return _

    for i, finish in enumerate((finish_k, finish_v)):
        pltpu.make_async_copy(part.at[i], part.at[i], recv_part.at[i]).wait()
        lax.fori_loop(0, heads, finish, None)

    pltpu.make_async_copy(sh_all, sh_all, recv_small.at[3]).wait()
    dp_all[dp] = sh_all[:, 0, :]

    def send_dp(i, _):
        @pl.when(i != dp)
        def _():
            pltpu.make_async_remote_copy(
                dp_all.at[dp],
                dp_all.at[dp],
                send_small.at[3],
                recv_small.at[4],
                device_id=(i, c),
                device_id_type=MESH,
            ).start()

        return _

    lax.fori_loop(0, dps, send_dp, None)
    others = dp_all.at[pl.ds(0, dps - 1)]
    pltpu.make_async_copy(others, others, recv_small.at[4]).wait()
    total = dp_all[0]
    for i in range(1, dps):
        total = total + dp_all[i]
    lane = lax.broadcasted_iota(jnp.int32, total.shape, 1)
    row = lax.broadcasted_iota(jnp.int32, total.shape, 0)
    ds_ref[...] = jnp.sum(jnp.where(lane == row, total, 0.0), axis=0, keepdims=True)[:, :heads]

    pltpu.make_async_copy(others, others, send_small.at[3]).wait()
    for i, ref in enumerate((kx, vx)):
        pltpu.make_async_copy(ref.at[s], ref.at[s], send_relay.at[i]).wait()
    for i in range(2):
        pltpu.make_async_copy(part.at[i], part.at[i], send_part.at[i]).wait()

    def drain(count):
        few = qg.at[pl.ds(0, count)]
        pltpu.make_async_copy(few, few, send_in).wait()
        pltpu.make_async_copy(few, few, send_in).wait()
        pltpu.make_async_copy(few, few, send_oq).wait()
        pltpu.make_async_copy(few, few, send_dkv).wait()
        tiles = sh_all.at[pl.ds(0, count)]
        pltpu.make_async_copy(tiles, tiles, send_small.at[2]).wait()

    @pl.when(same)
    def _():
        drain(heads - 1)

    @pl.when(jnp.logical_not(same))
    def _():
        drain(heads)

    for i, ref in enumerate((o_ref, dq_ref, dk_ref, dv_ref)):
        pltpu.make_async_copy(ref, ref, recv_out.at[i]).wait()


def settle_kernel(*refs):
    ins, outs, sems, last = refs[:5], refs[5:10], refs[10], refs[11]
    pieces = sems.shape[1]
    copies = [pltpu.make_async_copy(ins[4], outs[4], last)]
    for a, (src, dst) in enumerate(zip(ins[:4], outs[:4])):
        rows = src.shape[0] // pieces
        for i in range(pieces):
            part = pl.ds(i * rows, rows)
            copies.append(pltpu.make_async_copy(src.at[part], dst.at[part], sems.at[a, i]))
    for copy in copies:
        copy.start()
    for copy in copies:
        copy.wait()


def settle(*arrays):
    return pl.pallas_call(
        settle_kernel,
        out_shape=[jax.ShapeDtypeStruct(x.shape, x.dtype) for x in arrays],
        in_specs=[pl.BlockSpec(memory_space=pltpu.VMEM)] * 5,
        out_specs=[pl.BlockSpec(memory_space=pltpu.HBM)] * 5,
        scratch_shapes=[pltpu.SemaphoreType.DMA((4, 2)), pltpu.SemaphoreType.DMA],
        compiler_params=pltpu.CompilerParams(vmem_limit_bytes=6 * 2**20),
        name="settle",
    )(*arrays)


def per_device(queries, keys, values, sharpness, listing, adjoint):
    chips = lax.axis_size("seq")
    dps = lax.axis_size("dp")
    heads = chips // 2
    rows, features = queries.shape[1:]
    f32 = jnp.float32
    anywhere = pl.BlockSpec(memory_space=pl.ANY)
    block = (BLOCK, HD)
    whole = jax.ShapeDtypeStruct((rows, features), f32)
    dma = pltpu.SemaphoreType.DMA
    o, dq, dk, dv, ds = pl.pallas_call(
        functools.partial(kernel, chips, dps),
        out_shape=[whole] * 4 + [jax.ShapeDtypeStruct((1, heads), f32)],
        in_specs=[pl.BlockSpec(memory_space=pltpu.HBM)] * 6,
        out_specs=[anywhere] * 4 + [pl.BlockSpec(memory_space=pltpu.VMEM)],
        scratch_shapes=[
            pltpu.VMEM((2, heads) + block, f32),
            pltpu.VMEM((2, heads) + block, f32),
            pltpu.VMEM((heads, 2) + block, f32),
            pltpu.VMEM((heads, 2) + block, f32),
            pltpu.VMEM((2, heads) + block, f32),
            pltpu.VMEM((2, heads) + block, f32),
            pltpu.VMEM((heads,) + block, f32),
            pltpu.VMEM((heads,) + block, f32),
            pltpu.VMEM((2, heads) + block, f32),
            pltpu.VMEM((2, NB, chips), jnp.int32),
            pltpu.SMEM((NB, chips), jnp.int32),
            pltpu.SMEM((heads,), f32),
            pltpu.SMEM((heads,), jnp.int32),
            pltpu.SMEM((chips,), jnp.int32),
            pltpu.VMEM((8, HD), f32),
            pltpu.VMEM((8, HD), f32),
            pltpu.VMEM((8, HD), f32),
            pltpu.VMEM((heads, 8, HD), f32),
            pltpu.VMEM((dps, heads, HD), f32),
            dma,
            dma((2,)),
            dma,
            dma,
            dma((2,)),
            dma((4,)),
            dma((2,)),
            dma((heads,)),
            dma((2,)),
            dma((2,)),
            dma((4,)),
            dma((6,)),
        ],
        compiler_params=pltpu.CompilerParams(
            collective_id=0, has_side_effects=True, vmem_limit_bytes=48 * 2**20
        ),
        name="attend",
    )(
        *(
            pltpu.with_memory_space_constraint(x, pltpu.HBM)
            for x in (queries[0], keys[0], values[0], adjoint[0], listing[0].T, sharpness)
        )
    )
    o, dq, dk, dv, ds = settle(o, dq, dk, dv, ds)
    return o[None], dq[None], dk[None], dv[None], ds[0]


def solution(mesh):
    tokens = P("dp", "seq", None)
    return jax.shard_map(
        per_device,
        mesh=mesh,
        in_specs=(tokens, tokens, tokens, P(), P("dp", None, None), tokens),
        out_specs=(tokens, tokens, tokens, tokens, P()),
        check_vma=False,
    )
```
